32 devices in a mesh: site: 4 (over y, x), blk: 8 (over z, core).
Axes of the slice: x: 2, y: 2, z: 4, core: 2. Of those that a mesh axis runs over, the one named last changes fastest.
Arguments:
- corner: bfloat16 [4, 768, 768], P('site', 'blk'), may hold values from -6 to 6
- edge: bfloat16 [4, 768, 64, 768], P('site', 'blk'), may hold values from -0.02734375 to 0.02734375
- proj_left: bfloat16 [4, 768, 64, 768], P('site', 'blk'), may hold values from -0.21875 to 0.21875
- proj_right: bfloat16 [4, 768, 64, 768], P('site', 'blk'), may hold values from -0.21875 to 0.21875
- charge: int32 [4, 768], P('site'), may hold values from 0 to 15, never falling along the last dimension, each value on 1 to 96 neighbouring positions
- cot_left: float32 [4, 768, 768], P('site', 'blk'), may hold values from -2 to 2
- cot_right: float32 [4, 768, 768], P('site', 'blk'), may hold values from -2 to 2
Outputs:
- new_left: bfloat16 [4, 768, 768], P('site', 'blk')
- new_right: bfloat16 [4, 768, 768], P('site', 'blk')
- grad_left: bfloat16 [4, 768, 64, 768], P('site', 'blk')
- grad_right: bfloat16 [4, 768, 64, 768], P('site', 'blk')
The draws below stay inside these ranges and needn't reach their ends.
Inputs may be any that keep to these rules, and one draw needn't show every extreme that they name: `charge`: sector labels never fall along the bond index; each sector holds 1 to 96 indices.
All inputs are finite; a program needn't handle non-finite values.
Results may differ from the reference program's by a relative error of at most 0.0059.
Values may be sent and summed in bfloat16 or wider, within the bound.
A program may use at most 128 MiB of HBM per device.

```python
import math
import jax
import jax.numpy as jnp
import numpy as np
from jax import lax

CHI = 768
DD = 64
NSEC = 16
ITERS = 2
SITES = 4


def block_scale(key, shape, shards, least, largest):
    level = 1.0
    for axis_at, parts in shards:
        heights = jax.random.uniform(jax.random.fold_in(jax.random.fold_in(key, 6), axis_at), (parts,), jnp.float32, least / len(shards), largest / len(shards))
        level = level * jnp.repeat(jnp.exp(heights), shape[axis_at] // parts).reshape((-1,) + (1,) * (len(shape) - 1 - axis_at))
    return level


def profile(number_of, total, limit, skew):
    loads = [(1 << 20) // math.isqrt(rank ** skew) + 1 for rank in range(2, number_of + 1)]
    spare, holding = total - limit - (number_of - 1), [1] * (number_of - 1)
    while spare > 0:
        free = [i for i in range(number_of - 1) if holding[i] < limit]
        whole, budget = sum([loads[i] for i in free]), spare
        for i in free:
            more = min(limit - holding[i], max(1, budget * loads[i] // whole), spare)
            holding[i] = holding[i] + more
            spare = spare - more
    return np.array([limit] + holding)


def ragged(own_key, count, total, bound, skew):
    if count == 2:
        one = jax.random.randint(own_key, (), max(1, total - bound), min(bound, total - 1) + 1)
        return jnp.stack([one, total - one])
    tallies = jnp.asarray(profile(count, total, bound, skew), jnp.int32)
    pairs = (count - 1) // 2
    giver, taker = tallies[1:1 + 2 * pairs:2], tallies[2:2 + 2 * pairs:2]
    room = jnp.minimum(giver - 1, bound - taker)
    passed = jax.random.randint(jax.random.fold_in(own_key, 1), (pairs,), 0, 1 << 20) % (room + 1)
    tallies = tallies.at[1:1 + 2 * pairs:2].set(giver - passed).at[2:2 + 2 * pairs:2].set(taker + passed)
    return tallies[jax.random.permutation(jax.random.fold_in(own_key, 2), count)]


def centred(rng, dims, deviation, limit, pieces=(), dtype=jnp.bfloat16):
    factor_of = block_scale(rng, dims, pieces, -0.22, 0.18) if pieces else 1.0
    drawn = jax.random.normal(rng, dims, jnp.float32) * deviation * factor_of
    return jnp.minimum(jnp.maximum(drawn, -limit), limit).astype(dtype)


def setup_inputs(seed: int = 0) -> dict:
    splits = jax.random.split(jax.random.key(seed), 8)
    corner = centred(splits[0], (SITES, CHI, CHI), 1.0, 6.0, ((0, 4), (1, 8)))
    edge = centred(splits[1], (SITES, CHI, DD, CHI), (CHI * DD) ** -0.5, 0.02734375, ((0, 4), (1, 8)))
    proj_left = centred(splits[2], (SITES, CHI, DD, CHI), CHI ** -0.5, 0.21875, ((0, 4), (1, 8)))
    proj_right = centred(splits[3], (SITES, CHI, DD, CHI), CHI ** -0.5, 0.21875, ((0, 4), (1, 8)))
    charge = jax.vmap(lambda own: jnp.searchsorted(jnp.cumsum(ragged(own, NSEC, CHI, CHI // 8, 2)), jnp.arange(CHI), side="right"))(jax.random.split(splits[4], SITES)).reshape((SITES, CHI)).astype(jnp.int32)
    cot_left = centred(splits[5], (SITES, CHI, CHI), 0.25, 2.0, ((0, 4), (1, 8)), jnp.float32)
    cot_right = centred(splits[6], (SITES, CHI, CHI), 0.25, 2.0, ((0, 4), (1, 8)), jnp.float32)
    return dict(corner=corner, edge=edge, proj_left=proj_left, proj_right=proj_right, charge=charge, cot_left=cot_left, cot_right=cot_right)


def contract_first(left, right):
    return lax.dot_general(left, right, (((0,), (0,)), ((), ())), preferred_element_type=jnp.float32)


def contract_last(left, right):
    return lax.dot_general(left, right, (((1,), (1,)), ((), ())), preferred_element_type=jnp.float32)


def reference(corner, edge, proj_left, proj_right, charge, cot_left, cot_right):
    count_sites = corner.shape[0]
    prev_corner = jnp.roll(corner, 1, axis=0)
    next_corner = jnp.roll(corner, -1, axis=0)
    mask = (charge[:, :, None] == charge[:, None, :]).astype(jnp.float32)
    edge_flat = edge.reshape(count_sites, CHI * DD, CHI)
    left_flat = proj_left.reshape(count_sites, CHI * DD, CHI)
    right_flat = proj_right.reshape(count_sites, CHI * DD, CHI)
    enl_left = jnp.stack([contract_first(edge_flat[s], left_flat[s]).astype(jnp.bfloat16) for s in range(count_sites)])
    enl_right = jnp.stack([contract_first(edge_flat[s], right_flat[s]).astype(jnp.bfloat16) for s in range(count_sites)])
    new_left = jnp.stack([(mask[s] * jnp.dot(prev_corner[s], enl_left[s], preferred_element_type=jnp.float32)).astype(jnp.bfloat16) for s in range(count_sites)])
    new_right = jnp.stack([(mask[s] * jnp.dot(next_corner[s], enl_right[s], preferred_element_type=jnp.float32)).astype(jnp.bfloat16) for s in range(count_sites)])
    adj_left = cot_left
    adj_right = cot_right
    for step in range(ITERS):
        w_left = (mask * adj_left).astype(jnp.bfloat16)
        w_right = (mask * adj_right).astype(jnp.bfloat16)
        back_left = jnp.stack([contract_last(w_left[s], enl_left[s]) for s in range(count_sites)])
        back_right = jnp.stack([contract_last(w_right[s], enl_right[s]) for s in range(count_sites)])
        adj_left = cot_left + jnp.roll(back_left, -1, axis=0)
        adj_right = cot_right + jnp.roll(back_right, 1, axis=0)
    w_left = (mask * adj_left).astype(jnp.bfloat16)
    w_right = (mask * adj_right).astype(jnp.bfloat16)
    grads_left = []
    grads_right = []
    for s in range(count_sites):
        mid_left = contract_first(prev_corner[s], w_left[s]).astype(jnp.bfloat16)
        mid_right = contract_first(next_corner[s], w_right[s]).astype(jnp.bfloat16)
        grads_left.append(jnp.dot(edge_flat[s], mid_left, preferred_element_type=jnp.float32).astype(jnp.bfloat16).reshape(CHI, DD, CHI))
        grads_right.append(jnp.dot(edge_flat[s], mid_right, preferred_element_type=jnp.float32).astype(jnp.bfloat16).reshape(CHI, DD, CHI))
    return new_left, new_right, jnp.stack(grads_left), jnp.stack(grads_right)
```

```python
import functools

import jax
import jax.numpy as jnp
from jax import lax
from jax.experimental import pallas as pl
from jax.experimental.pallas import tpu as pltpu
from jax.sharding import PartitionSpec as P

ITERS = 2
LANES = 128
STEPS = 8
F32 = jnp.float32
BF16 = jnp.bfloat16


def dot(left, right, dims):
    return lax.dot_general(left, right, (dims, ((), ())), preferred_element_type=F32)


def chain_kernel(
    nsite, nblk, steps,
    corner, edge, left, right, labels, cot_left, cot_right,
    mids, new_left, new_right,
    acc, snd, rcv, enl, cland, cfull, lab_in, lab_dst, col_own, col_dst, cotf, wsend, cpair,
    wzero, wfull, part, got, newp, newgot, mid_got,
    c_s, c_r, l_s, l_r, w_s, w_r, p_s, p_r, e_s, e_r, r_s, r_r, a_s, a_r, n_s, n_r, m_s, m_r,
):
    step = pl.program_id(0)
    rows, width = corner.shape
    nz = nblk // 2
    pair = 2 * rows
    aligned = rows % 16 == 0
    blocks = width // LANES
    site = lax.axis_index("site")
    blk = lax.axis_index("blk")
    side = blk % 2
    z = blk // 2
    up = (site + 1) % nsite
    down = (site + nsite - 1) % nsite
    dest = (site + nsite - 1 + 2 * side) % nsite
    origin = (site + nsite + 1 - 2 * side) % nsite
    partner = 2 * z + 1 - side

    def copy(src, dst, send, recv, to_site, to_blk):
        return pltpu.make_async_remote_copy(
            src_ref=src, dst_ref=dst, send_sem=send, recv_sem=recv,
            device_id={"site": to_site, "blk": to_blk}, device_id_type=pl.DeviceIdType.MESH,
        )

    def own_rows(index):
        return pl.ds(pl.multiple_of(index * rows, rows), rows)

    def pair_rows(index):
        return pl.ds(pl.multiple_of(index * pair, pair), pair)

    def corner_slot(index):
        return cfull.at[own_rows(index)] if aligned else cland.at[index]

    def corner_copies():
        there = corner_slot(blk)
        out = []
        for p in range(nz):
            out.append(copy(corner, there, c_s.at[0, p], c_r.at[blk], up, 2 * p))
            out.append(copy(corner, there, c_s.at[1, p], c_r.at[blk], down, 2 * p + 1))
        return out

    def w_copies():
        out = []
        for d in range(1, nblk):
            to = (blk + d) % nblk
            out.append(copy(wsend.at[to % 2], wzero.at[own_rows(blk)], w_s.at[d], w_r.at[blk], site, to))
        return out

    def label_copy():
        return copy(lab_in, lab_dst, l_s, l_r, origin, blk)

    def cot_copy():
        return copy(cotf.at[1 - side], cpair.at[own_rows(side)], p_s, p_r, site, partner)

    def columns(lab, col):
        for i in range(blocks):
            at = slice(i * LANES, (i + 1) * LANES)
            col[at, :] = jnp.broadcast_to(lab[0:1, at].astype(F32), (LANES, LANES)).T

    def same(col_block, lab, j):
        return col_block == lab[0:1, j * LANES:(j + 1) * LANES].astype(F32)

    @pl.when(step == 0)
    def _():
        barrier = pltpu.get_barrier_semaphore()
        for where in (down, up):
            for b in range(nblk):
                pl.semaphore_signal(barrier, inc=1, device_id={"site": where, "blk": b}, device_id_type=pl.DeviceIdType.MESH)
        for d in range(1, nblk):
            pl.semaphore_signal(barrier, inc=1, device_id={"site": site, "blk": (blk + d) % nblk}, device_id_type=pl.DeviceIdType.MESH)
        pl.semaphore_wait(barrier, 3 * nblk - 1)
        lab_in[...] = labels[...]
        label_copy().start()
        columns(labels, col_own)
        mine = col_own[own_rows(blk), :]
        for s, cot in enumerate((cot_left, cot_right)):
            total = jnp.zeros((rows, LANES), F32)
            for j in range(blocks):
                total = total + jnp.where(same(mine, labels, j), cot[:, j * LANES:(j + 1) * LANES], 0.0)
            cotf[s] = total
            wsend[s] = total.astype(BF16).astype(wsend.dtype)
        cot_copy().start()
        for c in w_copies():
            c.start()
        for c in corner_copies():
            c.start()
        wzero[own_rows(blk), :] = wsend[side]
        cpair[own_rows(side), :] = cotf[side]
        acc[...] = jnp.zeros_like(acc)

    acc[0] += dot(edge[...], left[...], ((0,), (0,)))
    acc[1] += dot(edge[...], right[...], ((0,), (0,)))

    def window(i):
        return max(0, i - 1), min(blocks, i + 2)

    def back_partial(at):
        for i in range(blocks):
            rows_i = slice(i * LANES, (i + 1) * LANES)
            lo, hi = window(i)
            span = slice(lo * LANES, hi * LANES)
            folded = wzero[rows_i, :] if at == 0 else wfull[at - 1, rows_i, :]
            mine = col_own[rows_i, :]
            there = col_dst[rows_i, :]
            w = jnp.concatenate(
                [jnp.where(same(mine, labels, j), folded.astype(F32), 0.0) for j in range(lo, hi)], axis=1
            ).astype(BF16)
            back = dot(w, enl[span, span], ((1,), (1,)))
            total = jnp.zeros((LANES, LANES), F32)
            for j in range(lo, hi):
                piece = back[:, (j - lo) * LANES:(j - lo + 1) * LANES]
                total = total + jnp.where(same(there, lab_dst, j), piece, 0.0)
            part[at, rows_i, :] = total.astype(BF16)

    def reduce_copies(at):
        return [
            copy(part.at[at, slice_of(p)], got.at[at, z], r_s.at[at, p], r_r.at[at, z], dest, 2 * p + side)
            for p in range(nz)
        ]

    def slice_of(p):
        return pl.ds(p * pair, pair)

    def gather_copies(at):
        here = wfull.at[at, pair_rows(z)]
        return [
            copy(here, here, a_s.at[at, d], a_r.at[at, z], site, 2 * ((z + d) % nz) + side)
            for d in range(1, nz)
        ]

    def reduce_and_send(at):
        for q in range(nz):
            copy(got.at[at, q], got.at[at, q], r_s.at[at, q], r_r.at[at, q], dest, blk).wait_recv()
        total = cpair[...]
        for q in range(nz):
            total = total + got[at, q].astype(F32)
        wfull[at, pair_rows(z), :] = total.astype(BF16)
        for c in gather_copies(at):
            c.start()

    def gather_wait(at):
        for d in range(1, nz):
            src = (z + nz - d) % nz
            there = wfull.at[at, pair_rows(src)]
            copy(there, there, a_s.at[at, d], a_r.at[at, src], site, partner).wait_recv()

    def new_copies():
        out = []
        for d in range(1, nblk):
            to = (blk + d) % nblk
            out.append(copy(newp.at[own_rows(to)], newgot.at[blk], n_s.at[d], n_r.at[blk], site, to))
        return out

    @pl.when(step == steps - 1)
    def _():
        snd[...] = acc[1 - side].astype(BF16)
        swap = copy(snd, rcv, e_s, e_r, site, partner)
        swap.start()
        label_copy().wait_recv()
        columns(lab_dst, col_dst)
        cot_copy().wait_recv()
        for d in range(1, nblk):
            src = (blk + nblk - d) % nblk
            there = wzero.at[own_rows(src)]
            copy(there, there, w_s.at[d], w_r.at[src], site, partner).wait_recv()
        swap.wait_recv()
        enl[...] = (acc[side] + rcv[...].astype(F32)).astype(BF16)
        back_partial(0)
        for c in reduce_copies(0):
            c.start()
        for q in range(nblk):
            there = corner_slot(q)
            copy(there, there, c_s.at[0, 0], c_r.at[q], site, partner).wait_recv()
        if not aligned:
            for q in range(nz):
                both = [cland[2 * q].astype(F32), cland[2 * q + 1].astype(F32)]
                cfull[q * pair:(q + 1) * pair, :] = jnp.concatenate(both, axis=0).astype(BF16)
        for i in range(blocks):
            rows_i = slice(i * LANES, (i + 1) * LANES)
            lo, hi = window(i)
            fresh = dot(cfull[rows_i, :], enl[:, lo * LANES:hi * LANES], ((1,), (0,)))
            mine = col_own[rows_i, :]
            total = jnp.zeros((LANES, LANES), F32)
            for j in range(lo, hi):
                piece = fresh[:, (j - lo) * LANES:(j - lo + 1) * LANES]
                total = total + jnp.where(same(mine, labels, j), piece, 0.0)
            newp[rows_i, :] = total.astype(newp.dtype)
        reduce_and_send(0)
        for c in new_copies():
            c.start()
        newgot[blk] = newp[own_rows(blk), :]
        for at in range(1, ITERS):
            gather_wait(at - 1)
            back_partial(at)
            for c in reduce_copies(at):
                c.start()
            reduce_and_send(at)
        for d in range(1, nblk):
            src = (blk + nblk - d) % nblk
            copy(newgot.at[src], newgot.at[src], n_s.at[d], n_r.at[src], site, partner).wait_recv()
        mine = col_own[own_rows(blk), :]
        for s, out in enumerate((new_left, new_right)):
            total = jnp.zeros((rows, LANES), F32)
            for q in range(nz):
                total = total + newgot[2 * q + s].astype(F32)
            for j in range(blocks):
                out[:, j * LANES:(j + 1) * LANES] = jnp.where(same(mine, labels, j), total, 0.0).astype(BF16)
        gather_wait(ITERS - 1)
        for j in range(blocks):
            lo, hi = window(j)
            span = slice(lo * LANES, hi * LANES)
            w = jnp.where(same(col_own[span, :], labels, j), wfull[ITERS - 1, span, :].astype(F32), 0.0).astype(BF16)
            snd2 = dot(cfull[span, :], w, ((0,), (0,))).astype(BF16)
            mids[side, :, j * LANES:(j + 1) * LANES] = snd2
            enl[:, j * LANES:(j + 1) * LANES] = snd2
        last = copy(enl, mid_got, m_s, m_r, site, partner)
        last.start()
        last.wait_recv()
        mids[1 - side] = mid_got[...]
        last.wait_send()
        swap.wait_send()
        label_copy().wait_send()
        cot_copy().wait_send()
        for c in w_copies() + corner_copies() + new_copies():
            c.wait_send()
        for at in range(ITERS):
            for c in reduce_copies(at) + gather_copies(at):
                c.wait_send()


def grad_kernel(edge, mids, grad_left, grad_right):
    grad_left[...] = dot(edge[...], mids[0], ((1,), (0,))).astype(BF16)
    grad_right[...] = dot(edge[...], mids[1], ((1,), (0,))).astype(BF16)


def body(nsite, nblk, corner, edge, proj_left, proj_right, charge, cot_left, cot_right):
    rows, width = corner.shape[1:]
    depth = edge.shape[2]
    nz = nblk // 2
    pair = 2 * rows
    deep = rows * depth
    chunk = deep // STEPS
    edge_flat = edge[0].reshape(deep, width)
    left_flat = proj_left[0].reshape(deep, width)
    right_flat = proj_right[0].reshape(deep, width)
    labels = jnp.broadcast_to(charge, (8, width))

    def whole(*shape):
        return pl.BlockSpec(shape, lambda k: (0,) * len(shape))

    def piece():
        return pl.BlockSpec((chunk, width), lambda k: (k, 0))

    aligned = rows % 16 == 0
    small = BF16 if aligned else F32
    dma = pltpu.SemaphoreType.DMA
    mids, new_left, new_right = pl.pallas_call(
        functools.partial(chain_kernel, nsite, nblk, STEPS),
        grid=(STEPS,),
        out_shape=(
            jax.ShapeDtypeStruct((2, width, width), BF16),
            jax.ShapeDtypeStruct((rows, width), BF16),
            jax.ShapeDtypeStruct((rows, width), BF16),
        ),
        in_specs=[
            whole(rows, width), piece(), piece(), piece(), whole(8, width),
            whole(rows, width), whole(rows, width),
        ],
        out_specs=(whole(2, width, width), whole(rows, width), whole(rows, width)),
        scratch_shapes=[
            pltpu.VMEM((2, width, width), F32),
            pltpu.VMEM((width, width), BF16),
            pltpu.VMEM((width, width), BF16),
            pltpu.VMEM((width, width), BF16),
            pltpu.VMEM((1, 16, LANES) if aligned else (nblk, rows, width), BF16),
            pltpu.VMEM((width, width), BF16),
            pltpu.VMEM((8, width), jnp.int32),
            pltpu.VMEM((8, width), jnp.int32),
            pltpu.VMEM((width, LANES), F32),
            pltpu.VMEM((width, LANES), F32),
            pltpu.VMEM((2, rows, LANES), F32),
            pltpu.VMEM((2, rows, LANES), small),
            pltpu.VMEM((pair, LANES), F32),
            pltpu.VMEM((width, LANES), small),
            pltpu.VMEM((ITERS, width, LANES), BF16),
            pltpu.VMEM((ITERS, width, LANES), BF16),
            pltpu.VMEM((ITERS, nz, pair, LANES), BF16),
            pltpu.VMEM((width, LANES), small),
            pltpu.VMEM((nblk, rows, LANES), small),
            pltpu.VMEM((width, width), BF16),
            dma((2, nz)), dma((nblk,)),
            dma(()), dma(()),
            dma((nblk,)), dma((nblk,)),
            dma(()), dma(()),
            dma(()), dma(()),
            dma((ITERS, nz)), dma((ITERS, nz)),
            dma((ITERS, nz)), dma((ITERS, nz)),
            dma((nblk,)), dma((nblk,)),
            dma(()), dma(()),
        ],
        compiler_params=pltpu.CompilerParams(
            collective_id=0, has_side_effects=True, vmem_limit_bytes=52 * 1024 * 1024,
            dimension_semantics=("arbitrary",),
        ),
    )(corner[0], edge_flat, left_flat, right_flat, labels, cot_left[0], cot_right[0])
    grad_left, grad_right = pl.pallas_call(
        grad_kernel,
        grid=(STEPS,),
        out_shape=(jax.ShapeDtypeStruct((deep, width), BF16),) * 2,
        in_specs=[piece(), whole(2, width, width)],
        out_specs=(piece(), piece()),
        compiler_params=pltpu.CompilerParams(
            vmem_limit_bytes=48 * 1024 * 1024, dimension_semantics=("arbitrary",)
        ),
    )(edge_flat, mids)
    shape = (1, rows, depth, width)
    return (new_left[None], new_right[None], grad_left.reshape(shape), grad_right.reshape(shape))


def solution(mesh):
    placed = (
        P("site", "blk", None),
        P("site", "blk", None, None),
        P("site", "blk", None, None),
        P("site", "blk", None, None),
        P("site", None),
        P("site", "blk", None),
        P("site", "blk", None),
    )
    return jax.shard_map(
        functools.partial(body, mesh.shape["site"], mesh.shape["blk"]),
        mesh=mesh,
        in_specs=placed,
        out_specs=(
            P("site", "blk", None),
            P("site", "blk", None),
            P("site", "blk", None, None),
            P("site", "blk", None, None),
        ),
        check_vma=False,
    )
```

```python
import functools

import jax
import jax.numpy as jnp
from jax import lax
from jax.experimental import pallas as pl
from jax.experimental.pallas import tpu as pltpu
from jax.sharding import PartitionSpec as P

ITERS = 2
LANES = 128
VMEM = 60 * 1024 * 1024
F32 = jnp.float32
BF16 = jnp.bfloat16


def dot(left, right, dims):
    return lax.dot_general(left, right, (dims, ((), ())), preferred_element_type=F32)


def chain_kernel(
    nsite, nblk, steps,
    corner, edge, left, right, labels, cot_left, cot_right,
    mids, fresh_out,
    ebuf, pbuf, acc, snd, rcv, enl, cland, cfull, lab_in, lab_dst, col_own, col_dst, cotf, wsend, cpair,
    wzero, wfull, part, got, newp, newgot, mid_got,
    f_s, c_s, c_r, l_s, l_r, w_s, w_r, p_s, p_r, e_s, e_r, r_s, r_r, a_s, a_r, n_s, n_r, m_s, m_r,
):
    step = pl.program_id(0)
    rows, width = corner.shape
    nz = nblk // 2
    pair = 2 * rows
    chunk = edge.shape[0]
    aligned = rows % 16 == 0
    blocks = width // LANES
    site = lax.axis_index("site")
    blk = lax.axis_index("blk")
    side = blk % 2
    z = blk // 2
    up = (site + 1) % nsite
    down = (site + nsite - 1) % nsite
    dest = (site + nsite - 1 + 2 * side) % nsite
    origin = (site + nsite + 1 - 2 * side) % nsite
    partner = 2 * z + 1 - side

    def copy(src, dst, send, recv, to_site, to_blk):
        return pltpu.make_async_remote_copy(
            src_ref=src, dst_ref=dst, send_sem=send, recv_sem=recv,
            device_id={"site": to_site, "blk": to_blk}, device_id_type=pl.DeviceIdType.MESH,
        )

    def own_rows(index):
        return pl.ds(pl.multiple_of(index * rows, rows), rows)

    def pair_rows(index):
        return pl.ds(pl.multiple_of(index * pair, pair), pair)

    def corner_slot(index):
        return cfull.at[own_rows(index)] if aligned else cland.at[index]

    def corner_copies():
        there = corner_slot(blk)
        out = []
        for p in range(nz):
            out.append(copy(corner, there, c_s.at[0, p], c_r.at[blk], up, 2 * p))
            out.append(copy(corner, there, c_s.at[1, p], c_r.at[blk], down, 2 * p + 1))
        return out

    def w_copies():
        out = []
        for d in range(1, nblk):
            to = (blk + d) % nblk
            out.append(copy(wsend.at[to % 2], wzero.at[own_rows(blk)], w_s.at[d], w_r.at[blk], site, to))
        return out

    def label_copy():
        return copy(lab_in, lab_dst, l_s, l_r, origin, blk)

    def cot_copy():
        return copy(cotf.at[1 - side], cpair.at[own_rows(side)], p_s, p_r, site, partner)

    def columns(lab, col):
        for i in range(blocks):
            at = slice(i * LANES, (i + 1) * LANES)
            col[at, :] = jnp.broadcast_to(lab[0:1, at].astype(F32), (LANES, LANES)).T

    def same(col_block, lab, j):
        return col_block == lab[0:1, j * LANES:(j + 1) * LANES].astype(F32)

    def fetch(t):
        use_left = (t < steps) == (side == 1)
        here = pl.ds(pl.multiple_of(t % steps * chunk, chunk), chunk)

        @pl.when(use_left)
        def _():
            pltpu.make_async_copy(left.at[here], pbuf.at[t % 3], f_s.at[t % 3]).start()

        @pl.when(jnp.logical_not(use_left))
        def _():
            pltpu.make_async_copy(right.at[here], pbuf.at[t % 3], f_s.at[t % 3]).start()

    @pl.when(step == 0)
    def _():
        fetch(step)
        fetch(step + 1)
        barrier = pltpu.get_barrier_semaphore()
        for where in (down, up):
            for b in range(nblk):
                pl.semaphore_signal(barrier, inc=1, device_id={"site": where, "blk": b}, device_id_type=pl.DeviceIdType.MESH)
        for d in range(1, nblk):
            pl.semaphore_signal(barrier, inc=1, device_id={"site": site, "blk": (blk + d) % nblk}, device_id_type=pl.DeviceIdType.MESH)
        lab_in[...] = jnp.broadcast_to(labels[...], lab_in.shape)
        columns(lab_in, col_own)
        mine = col_own[own_rows(blk), :]
        for s, cot in enumerate((cot_left, cot_right)):
            total = jnp.zeros((rows, LANES), F32)
            for j in range(blocks):
                total = total + jnp.where(same(mine, lab_in, j), cot[:, j * LANES:(j + 1) * LANES], 0.0)
            cotf[s] = total
            wsend[s] = total.astype(BF16).astype(wsend.dtype)
        wzero[own_rows(blk), :] = wsend[side]
        cpair[own_rows(side), :] = cotf[side]
        acc[...] = jnp.zeros_like(acc)

    @pl.when(step == 1)
    def _():
        pl.semaphore_wait(pltpu.get_barrier_semaphore(), 3 * nblk - 1)
        label_copy().start()
        cot_copy().start()
        for c in w_copies() + corner_copies():
            c.start()

    @pl.when(step + 2 < 2 * steps)
    def _():
        fetch(step + 2)

    pltpu.make_async_copy(left.at[pl.ds(0, chunk)], pbuf.at[step % 3], f_s.at[step % 3]).wait()

    @pl.when(step < steps)
    def _():
        turned = edge[...].T
        ebuf[step] = turned
        acc[0] += dot(turned, pbuf[step % 3], ((1,), (0,)))

    @pl.when(step == steps)
    def _():
        snd[...] = acc[0].astype(BF16)
        copy(snd, rcv, e_s, e_r, site, partner).start()

    @pl.when(step >= steps)
    def _():
        acc[1] += dot(ebuf[step - steps], pbuf[step % 3], ((1,), (0,)))

    def window(i):
        return max(0, i - 1), min(blocks, i + 2)

    def back_partial(at):
        for i in range(blocks):
            rows_i = slice(i * LANES, (i + 1) * LANES)
            lo, hi = window(i)
            span = slice(lo * LANES, hi * LANES)
            folded = wzero[rows_i, :] if at == 0 else wfull[at - 1, rows_i, :]
            mine = col_own[rows_i, :]
            there = col_dst[rows_i, :]
            w = jnp.concatenate(
                [jnp.where(same(mine, lab_in, j), folded.astype(F32), 0.0) for j in range(lo, hi)], axis=1
            ).astype(BF16)
            back = dot(w, enl[span, span], ((1,), (1,)))
            total = jnp.zeros((LANES, LANES), F32)
            for j in range(lo, hi):
                piece = back[:, (j - lo) * LANES:(j - lo + 1) * LANES]
                total = total + jnp.where(same(there, lab_dst, j), piece, 0.0)
            part[at, rows_i, :] = total.astype(BF16)

    def reduce_copies(at):
        return [
            copy(part.at[at, slice_of(p)], got.at[at, z], r_s.at[at, p], r_r.at[at, z], dest, 2 * p + side)
            for p in range(nz)
        ]

    def slice_of(p):
        return pl.ds(p * pair, pair)

    def gather_copies(at):
        here = wfull.at[at, pair_rows(z)]
        return [
            copy(here, here, a_s.at[at, d], a_r.at[at, z], site, 2 * ((z + d) % nz) + side)
            for d in range(1, nz)
        ]

    def reduce_and_send(at):
        for q in range(nz):
            copy(got.at[at, q], got.at[at, q], r_s.at[at, q], r_r.at[at, q], dest, blk).wait_recv()
        total = cpair[...]
        for q in range(nz):
            total = total + got[at, q].astype(F32)
        wfull[at, pair_rows(z), :] = total.astype(BF16)
        for c in gather_copies(at):
            c.start()

    def gather_wait(at):
        for d in range(1, nz):
            src = (z + nz - d) % nz
            there = wfull.at[at, pair_rows(src)]
            copy(there, there, a_s.at[at, d], a_r.at[at, src], site, partner).wait_recv()

    def new_copies():
        out = []
        for d in range(1, nblk):
            to = (blk + d) % nblk
            out.append(copy(newp.at[own_rows(to)], newgot.at[blk], n_s.at[d], n_r.at[blk], site, to))
        return out

    def corner_wait():
        for q in range(nblk):
            there = corner_slot(q)
            copy(there, there, c_s.at[0, 0], c_r.at[q], site, partner).wait_recv()
        if not aligned:
            for q in range(nz):
                both = [cland[2 * q].astype(F32), cland[2 * q + 1].astype(F32)]
                cfull[q * pair:(q + 1) * pair, :] = jnp.concatenate(both, axis=0).astype(BF16)

    def new_partial():
        for i in range(blocks):
            rows_i = slice(i * LANES, (i + 1) * LANES)
            lo, hi = window(i)
            fresh = dot(cfull[rows_i, :], enl[:, lo * LANES:hi * LANES], ((1,), (0,)))
            mine = col_own[rows_i, :]
            total = jnp.zeros((LANES, LANES), F32)
            for j in range(lo, hi):
                piece = fresh[:, (j - lo) * LANES:(j - lo + 1) * LANES]
                total = total + jnp.where(same(mine, lab_in, j), piece, 0.0)
            newp[rows_i, :] = total.astype(newp.dtype)

    def mid_copy(j):
        here = slice(j * LANES, (j + 1) * LANES)
        return copy(enl.at[:, here], mid_got.at[:, here], m_s.at[j], m_r.at[j], site, partner)

    @pl.when(step == 2 * steps - 1)
    def _():
        label_copy().wait_recv()
        columns(lab_dst, col_dst)
        cot_copy().wait_recv()
        for d in range(1, nblk):
            src = (blk + nblk - d) % nblk
            there = wzero.at[own_rows(src)]
            copy(there, there, w_s.at[d], w_r.at[src], site, partner).wait_recv()
        swap = copy(snd, rcv, e_s, e_r, site, partner)
        swap.wait_recv()
        enl[...] = (acc[1] + rcv[...].astype(F32)).astype(BF16)
        for at in range(ITERS):
            if at:
                gather_wait(at - 1)
            back_partial(at)
            for c in reduce_copies(at):
                c.start()
            if at == ITERS - 1:
                corner_wait()
                new_partial()
                for c in new_copies():
                    c.start()
                newgot[blk] = newp[own_rows(blk), :]
            reduce_and_send(at)
        gather_wait(ITERS - 1)
        for j in range(blocks):
            lo, hi = window(j)
            span = slice(lo * LANES, hi * LANES)
            w = jnp.where(same(col_own[span, :], lab_in, j), wfull[ITERS - 1, span, :].astype(F32), 0.0).astype(BF16)
            piece = dot(cfull[span, :], w, ((0,), (0,))).astype(BF16)
            enl[:, j * LANES:(j + 1) * LANES] = piece
            mid_copy(j).start()
            mids[side, :, j * LANES:(j + 1) * LANES] = piece
        for d in range(1, nblk):
            src = (blk + nblk - d) % nblk
            copy(newgot.at[src], newgot.at[src], n_s.at[d], n_r.at[src], site, partner).wait_recv()
        for s in range(2):
            total = jnp.zeros((rows, LANES), F32)
            for q in range(nz):
                total = total + newgot[2 * q + s].astype(F32)
            fresh_out[s] = total
        fresh_out[2] = col_own[own_rows(blk), :]
        for j in range(blocks):
            mid_copy(j).wait_recv()
            mids[1 - side, :, j * LANES:(j + 1) * LANES] = mid_got[:, j * LANES:(j + 1) * LANES]
        swap.wait_send()
        label_copy().wait_send()
        cot_copy().wait_send()
        for j in range(blocks):
            mid_copy(j).wait_send()
        for c in w_copies() + corner_copies() + new_copies():
            c.wait_send()
        for at in range(ITERS):
            for c in reduce_copies(at) + gather_copies(at):
                c.wait_send()


def grad_kernel(edge, mids, fresh, labels, grad_left, grad_right, new_left, new_right):
    grad_left[...] = dot(edge[...], mids[0], ((1,), (0,))).astype(BF16)
    grad_right[...] = dot(edge[...], mids[1], ((1,), (0,))).astype(BF16)

    @pl.when(pl.program_id(0) == 0)
    def _():
        for s, out in enumerate((new_left, new_right)):
            for j in range(labels.shape[1] // LANES):
                at = slice(j * LANES, (j + 1) * LANES)
                keep = fresh[2] == labels[:, at].astype(F32)
                out[:, at] = jnp.where(keep, fresh[s], 0.0).astype(BF16)


def body(nsite, nblk, corner, edge, proj_left, proj_right, charge, cot_left, cot_right):
    rows, width = corner.shape[1:]
    depth = edge.shape[2]
    nz = nblk // 2
    pair = 2 * rows
    deep = rows * depth
    chunk = width if deep % width == 0 else deep // 8
    steps = deep // chunk
    edge_flat = edge[0].reshape(deep, width)
    left_flat = proj_left[0].reshape(deep, width)
    right_flat = proj_right[0].reshape(deep, width)

    def whole(*shape):
        return pl.BlockSpec(shape, lambda k: (0,) * len(shape))

    def piece():
        return pl.BlockSpec((chunk, width), lambda k: (jnp.minimum(k, steps - 1), 0))

    anywhere = pl.BlockSpec(memory_space=pl.ANY)

    aligned = rows % 16 == 0
    small = BF16 if aligned else F32
    dma = pltpu.SemaphoreType.DMA
    mids, fresh = pl.pallas_call(
        functools.partial(chain_kernel, nsite, nblk, steps),
        grid=(2 * steps,),
        out_shape=(
            jax.ShapeDtypeStruct((2, width, width), BF16),
            jax.ShapeDtypeStruct((3, rows, LANES), F32),
        ),
        in_specs=[
            whole(rows, width), piece(), anywhere, anywhere, whole(1, width),
            whole(rows, width), whole(rows, width),
        ],
        out_specs=(whole(2, width, width), whole(3, rows, LANES)),
        scratch_shapes=[
            pltpu.VMEM((steps, width, chunk), BF16),
            pltpu.VMEM((3, chunk, width), BF16),
            pltpu.VMEM((2, width, width), F32),
            pltpu.VMEM((width, width), BF16),
            pltpu.VMEM((width, width), BF16),
            pltpu.VMEM((width, width), BF16),
            pltpu.VMEM((1, 16, LANES) if aligned else (nblk, rows, width), BF16),
            pltpu.VMEM((width, width), BF16),
            pltpu.VMEM((8, width), jnp.int32),
            pltpu.VMEM((8, width), jnp.int32),
            pltpu.VMEM((width, LANES), F32),
            pltpu.VMEM((width, LANES), F32),
            pltpu.VMEM((2, rows, LANES), F32),
            pltpu.VMEM((2, rows, LANES), small),
            pltpu.VMEM((pair, LANES), F32),
            pltpu.VMEM((width, LANES), small),
            pltpu.VMEM((ITERS, width, LANES), BF16),
            pltpu.VMEM((ITERS, width, LANES), BF16),
            pltpu.VMEM((ITERS, nz, pair, LANES), BF16),
            pltpu.VMEM((width, LANES), small),
            pltpu.VMEM((nblk, rows, LANES), small),
            pltpu.VMEM((width, width), BF16),
            dma((3,)),
            dma((2, nz)), dma((nblk,)),
            dma(()), dma(()),
            dma((nblk,)), dma((nblk,)),
            dma(()), dma(()),
            dma(()), dma(()),
            dma((ITERS, nz)), dma((ITERS, nz)),
            dma((ITERS, nz)), dma((ITERS, nz)),
            dma((nblk,)), dma((nblk,)),
            dma((width // LANES,)), dma((width // LANES,)),
        ],
        compiler_params=pltpu.CompilerParams(
            collective_id=0, has_side_effects=True, vmem_limit_bytes=VMEM,
            dimension_semantics=("arbitrary",),
        ),
    )(corner[0], edge_flat, left_flat, right_flat, charge, cot_left[0], cot_right[0])
    grad_left, grad_right, new_left, new_right = pl.pallas_call(
        grad_kernel,
        grid=(steps,),
        out_shape=(jax.ShapeDtypeStruct((deep, width), BF16),) * 2
        + (jax.ShapeDtypeStruct((rows, width), BF16),) * 2,
        in_specs=[piece(), whole(2, width, width), whole(3, rows, LANES), whole(1, width)],
        out_specs=(piece(), piece(), whole(rows, width), whole(rows, width)),
        compiler_params=pltpu.CompilerParams(vmem_limit_bytes=VMEM, dimension_semantics=("arbitrary",)),
    )(edge_flat, mids, fresh, charge)
    shape = (1, rows, depth, width)
    return (new_left[None], new_right[None], grad_left.reshape(shape), grad_right.reshape(shape))


def solution(mesh):
    placed = (
        P("site", "blk", None),
        P("site", "blk", None, None),
        P("site", "blk", None, None),
        P("site", "blk", None, None),
        P("site", None),
        P("site", "blk", None),
        P("site", "blk", None),
    )
    return jax.shard_map(
        functools.partial(body, mesh.shape["site"], mesh.shape["blk"]),
        mesh=mesh,
        in_specs=placed,
        out_specs=(
            P("site", "blk", None),
            P("site", "blk", None),
            P("site", "blk", None, None),
            P("site", "blk", None, None),
        ),
        check_vma=False,
    )
```

```python
import functools

import jax
import jax.numpy as jnp
from jax import lax
from jax.experimental import pallas as pl
from jax.experimental.pallas import tpu as pltpu
from jax.sharding import PartitionSpec as P

ITERS = 2
LANES = 128
VMEM = 60 * 1024 * 1024
F32 = jnp.float32
BF16 = jnp.bfloat16


def dot(left, right, dims):
    return lax.dot_general(left, right, (dims, ((), ())), preferred_element_type=F32)


def chain_kernel(
    nsite, nblk, steps,
    corner, edge, left, right, labels, cot_left, cot_right,
    mids, fresh_out,
    ebuf, pbuf, acc, snd, rcv, enl, zland, cland, cfull, turned_corner, lab_in, lab_dst, col_own, col_dst, cotf, wsend, cpair,
    wzero, wfull, part, got, newp, newgot, mid_got,
    f_s, z_s, z_r, c_s, c_r, l_s, l_r, w_s, w_r, p_s, p_r, e_s, e_r, r_s, r_r, a_s, a_r, n_s, n_r, m_s, m_r,
):
    step = pl.program_id(0)
    rows, width = corner.shape
    nz = nblk // 2
    pair = 2 * rows
    chunk = edge.shape[0]
    aligned = rows % 16 == 0
    blocks = width // LANES
    site = lax.axis_index("site")
    blk = lax.axis_index("blk")
    side = blk % 2
    z = blk // 2
    up = (site + 1) % nsite
    down = (site + nsite - 1) % nsite
    dest = (site + nsite - 1 + 2 * side) % nsite
    origin = (site + nsite + 1 - 2 * side) % nsite
    partner = 2 * z + 1 - side

    def copy(src, dst, send, recv, to_site, to_blk):
        return pltpu.make_async_remote_copy(
            src_ref=src, dst_ref=dst, send_sem=send, recv_sem=recv,
            device_id={"site": to_site, "blk": to_blk}, device_id_type=pl.DeviceIdType.MESH,
        )

    def own_rows(index):
        return pl.ds(pl.multiple_of(index * rows, rows), rows)

    def pair_rows(index):
        return pl.ds(pl.multiple_of(index * pair, pair), pair)

    def corner_slot(index):
        return cfull.at[own_rows(index)] if aligned else cland.at[index]

    first = (site + side) % 2 == 1
    near = site + 1 - 2 * (site % 2)
    far = (site + nsite + 2 - 4 * ((site + jnp.where(first, 0, 1)) % 2)) % nsite

    def plane_copies():
        out = []
        for d in range(1, nz):
            to = 2 * ((z + d) % nz) + side
            out.append(copy(corner, zland.at[z], z_s.at[d], z_r.at[z], site, to))
        return out

    def near_copy(d):
        at = (z + d) % nz
        src = corner if d == 0 else zland.at[at]
        slot = 2 * at + side
        return copy(src, corner_slot(slot), c_s.at[0, d], c_r.at[slot], near, 2 * z + site % 2)

    def far_copies(d):
        out = []
        for c in range(2):
            slot = 2 * ((z + d) % nz) + c
            here = corner_slot(slot)
            out.append(copy(here, here, c_s.at[1 + c, d], c_r.at[slot], far, partner))
        return out

    def w_copies():
        out = []
        for d in range(1, nblk):
            to = (blk + d) % nblk
            out.append(copy(wsend.at[to % 2], wzero.at[own_rows(blk)], w_s.at[d], w_r.at[blk], site, to))
        return out

    def label_copy():
        return copy(lab_in, lab_dst, l_s, l_r, origin, blk)

    def cot_copy():
        return copy(cotf.at[1 - side], cpair.at[own_rows(side)], p_s, p_r, site, partner)

    def columns(lab, col):
        for i in range(blocks):
            at = slice(i * LANES, (i + 1) * LANES)
            col[at, :] = jnp.broadcast_to(lab[0:1, at].astype(F32), (LANES, LANES)).T

    def same(col_block, lab, j):
        return col_block == lab[0:1, j * LANES:(j + 1) * LANES].astype(F32)

    def fetch(t):
        use_left = (t < steps) == (side == 1)
        here = pl.ds(pl.multiple_of(t % steps * chunk, chunk), chunk)

        @pl.when(use_left)
        def _():
            pltpu.make_async_copy(left.at[here], pbuf.at[t % 3], f_s.at[t % 3]).start()

        @pl.when(jnp.logical_not(use_left))
        def _():
            pltpu.make_async_copy(right.at[here], pbuf.at[t % 3], f_s.at[t % 3]).start()

    @pl.when(step == 0)
    def _():
        fetch(step)
        fetch(step + 1)
        barrier = pltpu.get_barrier_semaphore()
        for where in (down, up):
            for b in range(nblk):
                pl.semaphore_signal(barrier, inc=1, device_id={"site": where, "blk": b}, device_id_type=pl.DeviceIdType.MESH)
        for d in range(1, nblk):
            pl.semaphore_signal(barrier, inc=1, device_id={"site": site, "blk": (blk + d) % nblk}, device_id_type=pl.DeviceIdType.MESH)
        pl.semaphore_signal(barrier, inc=1, device_id={"site": far, "blk": partner}, device_id_type=pl.DeviceIdType.MESH)
        lab_in[...] = jnp.broadcast_to(labels[...], lab_in.shape)
        columns(lab_in, col_own)
        mine = col_own[own_rows(blk), :]
        for s, cot in enumerate((cot_left, cot_right)):
            total = jnp.zeros((rows, LANES), F32)
            for j in range(blocks):
                total = total + jnp.where(same(mine, lab_in, j), cot[:, j * LANES:(j + 1) * LANES], 0.0)
            cotf[s] = total
            wsend[s] = total.astype(BF16).astype(wsend.dtype)
        wzero[own_rows(blk), :] = wsend[side]
        cpair[own_rows(side), :] = cotf[side]
        acc[...] = jnp.zeros_like(acc)

    @pl.when(step == 1)
    def _():
        pl.semaphore_wait(pltpu.get_barrier_semaphore(), 3 * nblk)
        label_copy().start()
        cot_copy().start()
        for c in w_copies() + plane_copies() + [near_copy(0)]:
            c.start()

    def relay_near(d):
        @pl.when(step == relay_step(d))
        def _():
            at = (z + d) % nz
            copy(zland.at[at], zland.at[at], z_s.at[d], z_r.at[at], site, partner).wait_recv()
            near_copy(d).start()

    def relay_far(d):
        @pl.when(jnp.logical_and(step == min(relay_step(d) + 3, 2 * steps - 1), first))
        def _():
            for c in range(2):
                slot = 2 * ((z + d) % nz) + c
                corner_wait(slot)
            for c in far_copies(d):
                c.start()

    def relay_step(d):
        return 2 + d * (2 * steps - 4) // nz

    def corner_wait(slot):
        there = corner_slot(slot)
        copy(there, there, c_s.at[0, 0], c_r.at[slot], site, partner).wait_recv()

    for d in range(1, nz):
        relay_near(d)
    for d in range(nz):
        relay_far(d)

    @pl.when(step + 2 < 2 * steps)
    def _():
        fetch(step + 2)

    pltpu.make_async_copy(left.at[pl.ds(0, chunk)], pbuf.at[step % 3], f_s.at[step % 3]).wait()

    @pl.when(step < steps)
    def _():
        turned = edge[...].T
        ebuf[step] = turned
        acc[0] += dot(turned, pbuf[step % 3], ((1,), (0,)))

    @pl.when(step == steps)
    def _():
        snd[...] = acc[0].astype(BF16)
        copy(snd, rcv, e_s, e_r, site, partner).start()

    @pl.when(step >= steps)
    def _():
        acc[1] += dot(ebuf[step - steps], pbuf[step % 3], ((1,), (0,)))

    def window(i):
        return max(0, i - 1), min(blocks, i + 2)

    def back_partial(at):
        for i in range(blocks):
            rows_i = slice(i * LANES, (i + 1) * LANES)
            lo, hi = window(i)
            span = slice(lo * LANES, hi * LANES)
            folded = wzero[rows_i, :] if at == 0 else wfull[at - 1, rows_i, :]
            mine = col_own[rows_i, :]
            there = col_dst[rows_i, :]
            w = jnp.concatenate(
                [jnp.where(same(mine, lab_in, j), folded.astype(F32), 0.0) for j in range(lo, hi)], axis=1
            ).astype(BF16)
            back = dot(w, enl[span, span], ((1,), (1,)))
            total = jnp.zeros((LANES, LANES), F32)
            for j in range(lo, hi):
                piece = back[:, (j - lo) * LANES:(j - lo + 1) * LANES]
                total = total + jnp.where(same(there, lab_dst, j), piece, 0.0)
            part[at, rows_i, :] = total.astype(BF16)

    def reduce_copies(at):
        return [
            copy(part.at[at, slice_of(p)], got.at[at, z], r_s.at[at, p], r_r.at[at, z], dest, 2 * p + side)
            for p in range(nz)
        ]

    def slice_of(p):
        return pl.ds(p * pair, pair)

    def gather_copies(at):
        here = wfull.at[at, pair_rows(z)]
        return [
            copy(here, here, a_s.at[at, d], a_r.at[at, z], site, 2 * ((z + d) % nz) + side)
            for d in range(1, nz)
        ]

    def reduce_and_send(at):
        for q in range(nz):
            copy(got.at[at, q], got.at[at, q], r_s.at[at, q], r_r.at[at, q], dest, blk).wait_recv()
        total = cpair[...]
        for q in range(nz):
            total = total + got[at, q].astype(F32)
        wfull[at, pair_rows(z), :] = total.astype(BF16)
        for c in gather_copies(at):
            c.start()

    def gather_wait(at):
        for d in range(1, nz):
            src = (z + nz - d) % nz
            there = wfull.at[at, pair_rows(src)]
            copy(there, there, a_s.at[at, d], a_r.at[at, src], site, partner).wait_recv()

    def new_copies():
        out = []
        for d in range(1, nblk):
            to = (blk + d) % nblk
            out.append(copy(newp.at[own_rows(to)], newgot.at[blk], n_s.at[d], n_r.at[blk], site, to))
        return out

    def corner_ready():
        @pl.when(jnp.logical_not(first))
        def _():
            for q in range(nblk):
                corner_wait(q)
        if not aligned:
            for q in range(nz):
                both = [cland[2 * q].astype(F32), cland[2 * q + 1].astype(F32)]
                cfull[q * pair:(q + 1) * pair, :] = jnp.concatenate(both, axis=0).astype(BF16)

    def new_partial():
        for i in range(blocks):
            rows_i = slice(i * LANES, (i + 1) * LANES)
            lo, hi = window(i)
            fresh = dot(cfull[rows_i, :], enl[:, lo * LANES:hi * LANES], ((1,), (0,)))
            mine = col_own[rows_i, :]
            total = jnp.zeros((LANES, LANES), F32)
            for j in range(lo, hi):
                piece = fresh[:, (j - lo) * LANES:(j - lo + 1) * LANES]
                total = total + jnp.where(same(mine, lab_in, j), piece, 0.0)
            newp[rows_i, :] = total.astype(newp.dtype)

    groups = [range(j, min(blocks, j + 2)) for j in range(0, blocks, 2)]

    def mid_copy(g):
        here = slice(g[0] * LANES, (g[-1] + 1) * LANES)
        return copy(enl.at[:, here], mid_got.at[:, here], m_s.at[g[0]], m_r.at[g[0]], site, partner)

    @pl.when(step == 2 * steps - 1)
    def _():
        label_copy().wait_recv()
        columns(lab_dst, col_dst)
        cot_copy().wait_recv()
        for d in range(1, nblk):
            src = (blk + nblk - d) % nblk
            there = wzero.at[own_rows(src)]
            copy(there, there, w_s.at[d], w_r.at[src], site, partner).wait_recv()
        swap = copy(snd, rcv, e_s, e_r, site, partner)
        swap.wait_recv()
        enl[...] = (acc[1] + rcv[...].astype(F32)).astype(BF16)
        for at in range(ITERS):
            if at:
                gather_wait(at - 1)
            back_partial(at)
            for c in reduce_copies(at):
                c.start()
            if at == ITERS - 1:
                corner_ready()
                turned_corner[...] = cfull[...].T
                new_partial()
                for c in new_copies():
                    c.start()
                newgot[blk] = newp[own_rows(blk), :]
            reduce_and_send(at)
        gather_wait(ITERS - 1)
        for g in groups:
            lo, hi = max(0, g[0] - 1), min(blocks, g[-1] + 2)
            span = slice(lo * LANES, hi * LANES)
            here = slice(g[0] * LANES, (g[-1] + 1) * LANES)
            last = wfull[ITERS - 1, span, :].astype(F32)
            mine = col_own[span, :]
            w = jnp.concatenate([jnp.where(same(mine, lab_in, j), last, 0.0) for j in g], axis=1).astype(BF16)
            piece = dot(turned_corner[:, span], w, ((1,), (0,))).astype(BF16)
            enl[:, here] = piece
            mid_copy(g).start()
            mids[side, :, here] = piece
        for d in range(1, nblk):
            src = (blk + nblk - d) % nblk
            copy(newgot.at[src], newgot.at[src], n_s.at[d], n_r.at[src], site, partner).wait_recv()
        for s in range(2):
            total = jnp.zeros((rows, LANES), F32)
            for q in range(nz):
                total = total + newgot[2 * q + s].astype(F32)
            fresh_out[s] = total
        fresh_out[2] = col_own[own_rows(blk), :]
        for g in groups:
            here = slice(g[0] * LANES, (g[-1] + 1) * LANES)
            mid_copy(g).wait_recv()
            mids[1 - side, :, here] = mid_got[:, here]
        swap.wait_send()
        label_copy().wait_send()
        cot_copy().wait_send()
        for g in groups:
            mid_copy(g).wait_send()
        for c in w_copies() + plane_copies() + new_copies():
            c.wait_send()
        for d in range(nz):
            near_copy(d).wait_send()

        @pl.when(first)
        def _():
            for d in range(nz):
                for c in far_copies(d):
                    c.wait_send()
        for at in range(ITERS):
            for c in reduce_copies(at) + gather_copies(at):
                c.wait_send()


def grad_kernel(edge, mids, fresh, labels, grad_left, grad_right, new_left, new_right):
    grad_left[...] = dot(edge[...], mids[0], ((1,), (0,))).astype(BF16)
    grad_right[...] = dot(edge[...], mids[1], ((1,), (0,))).astype(BF16)

    @pl.when(pl.program_id(0) == 0)
    def _():
        for s, out in enumerate((new_left, new_right)):
            for j in range(labels.shape[1] // LANES):
                at = slice(j * LANES, (j + 1) * LANES)
                keep = fresh[2] == labels[:, at].astype(F32)
                out[:, at] = jnp.where(keep, fresh[s], 0.0).astype(BF16)


def body(nsite, nblk, corner, edge, proj_left, proj_right, charge, cot_left, cot_right):
    rows, width = corner.shape[1:]
    depth = edge.shape[2]
    nz = nblk // 2
    pair = 2 * rows
    deep = rows * depth
    chunk = width if deep % width == 0 else deep // 8
    steps = deep // chunk
    edge_flat = edge[0].reshape(deep, width)
    left_flat = proj_left[0].reshape(deep, width)
    right_flat = proj_right[0].reshape(deep, width)

    def whole(*shape):
        return pl.BlockSpec(shape, lambda k: (0,) * len(shape))

    def piece():
        return pl.BlockSpec((chunk, width), lambda k: (jnp.minimum(k, steps - 1), 0))

    anywhere = pl.BlockSpec(memory_space=pl.ANY)

    aligned = rows % 16 == 0
    small = BF16 if aligned else F32
    dma = pltpu.SemaphoreType.DMA
    mids, fresh = pl.pallas_call(
        functools.partial(chain_kernel, nsite, nblk, steps),
        grid=(2 * steps,),
        out_shape=(
            jax.ShapeDtypeStruct((2, width, width), BF16),
            jax.ShapeDtypeStruct((3, rows, LANES), F32),
        ),
        in_specs=[
            whole(rows, width), piece(), anywhere, anywhere, whole(1, width),
            whole(rows, width), whole(rows, width),
        ],
        out_specs=(whole(2, width, width), whole(3, rows, LANES)),
        scratch_shapes=[
            pltpu.VMEM((steps, width, chunk), BF16),
            pltpu.VMEM((3, chunk, width), BF16),
            pltpu.VMEM((2, width, width), F32),
            pltpu.VMEM((width, width), BF16),
            pltpu.VMEM((width, width), BF16),
            pltpu.VMEM((width, width), BF16),
            pltpu.VMEM((nz, rows, width), BF16),
            pltpu.VMEM((1, 16, LANES) if aligned else (nblk, rows, width), BF16),
            pltpu.VMEM((width, width), BF16),
            pltpu.VMEM((width, width), BF16),
            pltpu.VMEM((8, width), jnp.int32),
            pltpu.VMEM((8, width), jnp.int32),
            pltpu.VMEM((width, LANES), F32),
            pltpu.VMEM((width, LANES), F32),
            pltpu.VMEM((2, rows, LANES), F32),
            pltpu.VMEM((2, rows, LANES), small),
            pltpu.VMEM((pair, LANES), F32),
            pltpu.VMEM((width, LANES), small),
            pltpu.VMEM((ITERS, width, LANES), BF16),
            pltpu.VMEM((ITERS, width, LANES), BF16),
            pltpu.VMEM((ITERS, nz, pair, LANES), BF16),
            pltpu.VMEM((width, LANES), small),
            pltpu.VMEM((nblk, rows, LANES), small),
            pltpu.VMEM((width, width), BF16),
            dma((3,)),
            dma((nz,)), dma((nz,)),
            dma((3, nz)), dma((nblk,)),
            dma(()), dma(()),
            dma((nblk,)), dma((nblk,)),
            dma(()), dma(()),
            dma(()), dma(()),
            dma((ITERS, nz)), dma((ITERS, nz)),
            dma((ITERS, nz)), dma((ITERS, nz)),
            dma((nblk,)), dma((nblk,)),
            dma((width // LANES,)), dma((width // LANES,)),
        ],
        compiler_params=pltpu.CompilerParams(
            collective_id=0, has_side_effects=True, vmem_limit_bytes=VMEM,
            dimension_semantics=("arbitrary",),
        ),
    )(corner[0], edge_flat, left_flat, right_flat, charge, cot_left[0], cot_right[0])
    grad_left, grad_right, new_left, new_right = pl.pallas_call(
        grad_kernel,
        grid=(steps,),
        out_shape=(jax.ShapeDtypeStruct((deep, width), BF16),) * 2
        + (jax.ShapeDtypeStruct((rows, width), BF16),) * 2,
        in_specs=[piece(), whole(2, width, width), whole(3, rows, LANES), whole(1, width)],
        out_specs=(piece(), piece(), whole(rows, width), whole(rows, width)),
        compiler_params=pltpu.CompilerParams(vmem_limit_bytes=VMEM, dimension_semantics=("arbitrary",)),
    )(edge_flat, mids, fresh, charge)
    shape = (1, rows, depth, width)
    return (new_left[None], new_right[None], grad_left.reshape(shape), grad_right.reshape(shape))


def solution(mesh):
    placed = (
        P("site", "blk", None),
        P("site", "blk", None, None),
        P("site", "blk", None, None),
        P("site", "blk", None, None),
        P("site", None),
        P("site", "blk", None),
        P("site", "blk", None),
    )
    return jax.shard_map(
        functools.partial(body, mesh.shape["site"], mesh.shape["blk"]),
        mesh=mesh,
        in_specs=placed,
        out_specs=(
            P("site", "blk", None),
            P("site", "blk", None),
            P("site", "blk", None, None),
            P("site", "blk", None, None),
        ),
        check_vma=False,
    )
```

```python
import functools

import jax
import jax.numpy as jnp
from jax import lax
from jax.experimental import pallas as pl
from jax.experimental.pallas import tpu as pltpu
from jax.sharding import PartitionSpec as P

ITERS = 2
LANES = 128
VMEM = 60 * 1024 * 1024
F32 = jnp.float32
BF16 = jnp.bfloat16


def dot(left, right, dims):
    return lax.dot_general(left, right, (dims, ((), ())), preferred_element_type=F32)


def chain_kernel(
    nsite, nblk, steps,
    corner, edge, left, right, labels, cot_left, cot_right,
    turned_out, w_out, col_out, fresh_out,
    ebuf, estore, tbuf, cother, wother, pbuf, acc, snd, rcv, enl, cland, cfull, lab_in, lab_dst, col_own, col_dst, cotf, wsend, cpair,
    wzero, wfull, part, got, newp, newgot,
    f_s, c_s, c_r, l_s, l_r, w_s, w_r, p_s, p_r, e_s, e_r, r_s, r_r, a_s, a_r, n_s, n_r, o_s, o_r, v_s, v_r, t_s,
):
    step = pl.program_id(0)
    rows, width = corner.shape
    nz = nblk // 2
    pair = 2 * rows
    chunk = edge.shape[0]
    aligned = rows % 16 == 0
    blocks = width // LANES
    site = lax.axis_index("site")
    blk = lax.axis_index("blk")
    side = blk % 2
    z = blk // 2
    up = (site + 1) % nsite
    down = (site + nsite - 1) % nsite
    dest = (site + nsite - 1 + 2 * side) % nsite
    origin = (site + nsite + 1 - 2 * side) % nsite
    partner = 2 * z + 1 - side

    def copy(src, dst, send, recv, to_site, to_blk):
        return pltpu.make_async_remote_copy(
            src_ref=src, dst_ref=dst, send_sem=send, recv_sem=recv,
            device_id={"site": to_site, "blk": to_blk}, device_id_type=pl.DeviceIdType.MESH,
        )

    def own_rows(index):
        return pl.ds(pl.multiple_of(index * rows, rows), rows)

    def pair_rows(index):
        return pl.ds(pl.multiple_of(index * pair, pair), pair)

    def corner_slot(index):
        return cfull.at[own_rows(index)] if aligned else cland.at[index]

    def corner_copies():
        there = corner_slot(blk)
        out = []
        for p in range(nz):
            out.append(copy(corner, there, c_s.at[0, p], c_r.at[blk], up, 2 * p))
            out.append(copy(corner, there, c_s.at[1, p], c_r.at[blk], down, 2 * p + 1))
        return out

    def w_copies():
        out = []
        for d in range(1, nblk):
            to = (blk + d) % nblk
            out.append(copy(wsend.at[to % 2], wzero.at[own_rows(blk)], w_s.at[d], w_r.at[blk], site, to))
        return out

    def label_copy():
        return copy(lab_in, lab_dst, l_s, l_r, origin, blk)

    def cot_copy():
        return copy(cotf.at[1 - side], cpair.at[own_rows(side)], p_s, p_r, site, partner)

    def columns(lab, col):
        for i in range(blocks):
            at = slice(i * LANES, (i + 1) * LANES)
            col[at, :] = jnp.broadcast_to(lab[0:1, at].astype(F32), (LANES, LANES)).T

    def same(col_block, lab, j):
        return col_block == lab[0:1, j * LANES:(j + 1) * LANES].astype(F32)

    def fetch(t):
        use_left = (t < steps) == (side == 1)
        here = pl.ds(pl.multiple_of(t % steps * chunk, chunk), chunk)

        @pl.when(use_left)
        def _():
            pltpu.make_async_copy(left.at[here], pbuf.at[t % 3], f_s.at[t % 3]).start()

        @pl.when(jnp.logical_not(use_left))
        def _():
            pltpu.make_async_copy(right.at[here], pbuf.at[t % 3], f_s.at[t % 3]).start()

    @pl.when(step == 0)
    def _():
        fetch(step)
        fetch(step + 1)
        barrier = pltpu.get_barrier_semaphore()
        for where in (down, up):
            for b in range(nblk):
                pl.semaphore_signal(barrier, inc=1, device_id={"site": where, "blk": b}, device_id_type=pl.DeviceIdType.MESH)
        for d in range(1, nblk):
            pl.semaphore_signal(barrier, inc=1, device_id={"site": site, "blk": (blk + d) % nblk}, device_id_type=pl.DeviceIdType.MESH)
        lab_in[...] = jnp.broadcast_to(labels[...], lab_in.shape)
        columns(lab_in, col_own)
        mine = col_own[own_rows(blk), :]
        for s, cot in enumerate((cot_left, cot_right)):
            total = jnp.zeros((rows, LANES), F32)
            for j in range(blocks):
                total = total + jnp.where(same(mine, lab_in, j), cot[:, j * LANES:(j + 1) * LANES], 0.0)
            cotf[s] = total
            wsend[s] = total.astype(BF16).astype(wsend.dtype)
        wzero[own_rows(blk), :] = wsend[side]
        cpair[own_rows(side), :] = cotf[side]
        acc[...] = jnp.zeros_like(acc)

    @pl.when(step == 1)
    def _():
        pl.semaphore_wait(pltpu.get_barrier_semaphore(), 3 * nblk - 1)
        label_copy().start()
        cot_copy().start()
        for c in w_copies() + corner_copies():
            c.start()

    @pl.when(step + 2 < 2 * steps)
    def _():
        fetch(step + 2)

    pltpu.make_async_copy(left.at[pl.ds(0, chunk)], pbuf.at[step % 3], f_s.at[step % 3]).wait()

    @pl.when(step < steps)
    def _():
        turned = edge[...].T
        ebuf[step] = turned
        estore[step] = edge[...]
        acc[0] += dot(turned, pbuf[step % 3], ((1,), (0,)))

    @pl.when(step == steps)
    def _():
        snd[...] = acc[0].astype(BF16)
        copy(snd, rcv, e_s, e_r, site, partner).start()

    @pl.when(step >= steps)
    def _():
        acc[1] += dot(ebuf[step - steps], pbuf[step % 3], ((1,), (0,)))

    def window(i):
        return max(0, i - 1), min(blocks, i + 2)

    def back_partial(at):
        for i in range(blocks):
            rows_i = slice(i * LANES, (i + 1) * LANES)
            lo, hi = window(i)
            span = slice(lo * LANES, hi * LANES)
            folded = wzero[rows_i, :] if at == 0 else wfull[at - 1, rows_i, :]
            mine = col_own[rows_i, :]
            there = col_dst[rows_i, :]
            w = jnp.concatenate(
                [jnp.where(same(mine, lab_in, j), folded.astype(F32), 0.0) for j in range(lo, hi)], axis=1
            ).astype(BF16)
            back = dot(w, enl[span, span], ((1,), (1,)))
            total = jnp.zeros((LANES, LANES), F32)
            for j in range(lo, hi):
                piece = back[:, (j - lo) * LANES:(j - lo + 1) * LANES]
                total = total + jnp.where(same(there, lab_dst, j), piece, 0.0)
            part[at, rows_i, :] = total.astype(BF16)

    def reduce_copies(at):
        return [
            copy(part.at[at, slice_of(p)], got.at[at, z], r_s.at[at, p], r_r.at[at, z], dest, 2 * p + side)
            for p in range(nz)
        ]

    def slice_of(p):
        return pl.ds(p * pair, pair)

    def gather_copies(at):
        here = wfull.at[at, pair_rows(z)]
        return [
            copy(here, here, a_s.at[at, d], a_r.at[at, z], site, 2 * ((z + d) % nz) + side)
            for d in range(1, nz)
        ]

    def reduce_and_send(at):
        for q in range(nz):
            copy(got.at[at, q], got.at[at, q], r_s.at[at, q], r_r.at[at, q], dest, blk).wait_recv()
        total = cpair[...]
        for q in range(nz):
            total = total + got[at, q].astype(F32)
        wfull[at, pair_rows(z), :] = total.astype(BF16)
        for c in gather_copies(at):
            c.start()

    def gather_wait(at):
        for d in range(1, nz):
            src = (z + nz - d) % nz
            there = wfull.at[at, pair_rows(src)]
            copy(there, there, a_s.at[at, d], a_r.at[at, src], site, partner).wait_recv()

    def new_copies():
        out = []
        for d in range(1, nblk):
            to = (blk + d) % nblk
            out.append(copy(newp.at[own_rows(to)], newgot.at[blk], n_s.at[d], n_r.at[blk], site, to))
        return out

    def corner_wait():
        for q in range(nblk):
            there = corner_slot(q)
            copy(there, there, c_s.at[0, 0], c_r.at[q], site, partner).wait_recv()
        if not aligned:
            for q in range(nz):
                both = [cland[2 * q].astype(F32), cland[2 * q + 1].astype(F32)]
                cfull[q * pair:(q + 1) * pair, :] = jnp.concatenate(both, axis=0).astype(BF16)

    def new_partial():
        for i in range(blocks):
            rows_i = slice(i * LANES, (i + 1) * LANES)
            lo, hi = window(i)
            fresh = dot(cfull[rows_i, :], enl[:, lo * LANES:hi * LANES], ((1,), (0,)))
            mine = col_own[rows_i, :]
            total = jnp.zeros((LANES, LANES), F32)
            for j in range(lo, hi):
                piece = fresh[:, (j - lo) * LANES:(j - lo + 1) * LANES]
                total = total + jnp.where(same(mine, lab_in, j), piece, 0.0)
            newp[rows_i, :] = total.astype(newp.dtype)

    halves = (range(0, steps // 2), range(steps // 2, steps))

    def store_copy(which, k, slot):
        return pltpu.make_async_copy(
            tbuf.at[slot], turned_out.at[which, pl.ds(k * chunk, chunk)], t_s.at[slot]
        )

    def edge_corner(which, full, chunks, before):
        for slot, k in enumerate(chunks):
            if before is not None and slot < len(before[1]):
                store_copy(before[0], before[1][slot], slot).wait()
            tbuf[slot] = dot(estore[k], full[...], ((1,), (1,))).astype(BF16)
            store_copy(which, k, slot).start()
        if before is not None:
            for slot in range(len(chunks), len(before[1])):
                store_copy(before[0], before[1][slot], slot).wait()

    @pl.when(step == 2 * steps - 1)
    def _():
        label_copy().wait_recv()
        columns(lab_dst, col_dst)
        cot_copy().wait_recv()
        for d in range(1, nblk):
            src = (blk + nblk - d) % nblk
            there = wzero.at[own_rows(src)]
            copy(there, there, w_s.at[d], w_r.at[src], site, partner).wait_recv()
        swap = copy(snd, rcv, e_s, e_r, site, partner)
        swap.wait_recv()
        enl[...] = (acc[1] + rcv[...].astype(F32)).astype(BF16)
        forward = copy(cfull, cother, o_s, o_r, site, partner)
        w_swap = copy(wfull.at[ITERS - 1], wother, v_s, v_r, site, partner)
        before = None
        for at in range(ITERS):
            if at:
                gather_wait(at - 1)
            back_partial(at)
            for c in reduce_copies(at):
                c.start()
            if at == 0:
                corner_wait()
                forward.start()
                edge_corner(side, cfull, halves[0], before)
                before = (side, halves[0])
            if at == ITERS - 1:
                forward.wait_recv()
                new_partial()
                for c in new_copies():
                    c.start()
                newgot[blk] = newp[own_rows(blk), :]
                edge_corner(1 - side, cother, halves[0], before)
                before = (1 - side, halves[0])
            reduce_and_send(at)
            if at == 0:
                edge_corner(side, cfull, halves[1], before)
                before = (side, halves[1])
            if at == ITERS - 1:
                edge_corner(1 - side, cother, halves[1], before)
                before = (1 - side, halves[1])
        gather_wait(ITERS - 1)
        w_swap.start()
        w_out[side] = wfull[ITERS - 1]
        col_out[...] = col_own[...]
        for d in range(1, nblk):
            src = (blk + nblk - d) % nblk
            copy(newgot.at[src], newgot.at[src], n_s.at[d], n_r.at[src], site, partner).wait_recv()
        for s in range(2):
            total = jnp.zeros((rows, LANES), F32)
            for q in range(nz):
                total = total + newgot[2 * q + s].astype(F32)
            fresh_out[s] = total
        fresh_out[2] = col_own[own_rows(blk), :]
        w_swap.wait_recv()
        w_out[1 - side] = wother[...]
        for slot, k in enumerate(before[1]):
            store_copy(before[0], k, slot).wait()
        w_swap.wait_send()
        forward.wait_send()
        swap.wait_send()
        label_copy().wait_send()
        cot_copy().wait_send()
        for c in w_copies() + corner_copies() + new_copies():
            c.wait_send()
        for at in range(ITERS):
            for c in reduce_copies(at) + gather_copies(at):
                c.wait_send()


def grad_kernel(turned, folded, column, fresh, labels, grad_left, grad_right, new_left, new_right, wide):
    blocks = labels.shape[1] // LANES
    groups = []
    for j in range(0, blocks, 2):
        top = min(blocks, j + 2)
        groups.append((slice(max(0, j - 1) * LANES, min(blocks, top + 1) * LANES), range(j, top)))

    @pl.when(pl.program_id(0) == 0)
    def _():
        for s in range(2):
            for span, inside in groups:
                for j in inside:
                    at = slice(j * LANES, (j + 1) * LANES)
                    keep = column[span, :] == labels[:, at].astype(F32)
                    wide[s, span, at] = jnp.where(keep, folded[s, span, :].astype(F32), 0.0).astype(BF16)

    for s, out in enumerate((grad_left, grad_right)):
        for span, inside in groups:
            here = slice(inside[0] * LANES, (inside[-1] + 1) * LANES)
            out[:, here] = dot(turned[s, :, span], wide[s, span, here], ((1,), (0,))).astype(BF16)

    @pl.when(pl.program_id(0) == 0)
    def _():
        for s, out in enumerate((new_left, new_right)):
            for j in range(labels.shape[1] // LANES):
                at = slice(j * LANES, (j + 1) * LANES)
                keep = fresh[2] == labels[:, at].astype(F32)
                out[:, at] = jnp.where(keep, fresh[s], 0.0).astype(BF16)


def body(nsite, nblk, corner, edge, proj_left, proj_right, charge, cot_left, cot_right):
    rows, width = corner.shape[1:]
    depth = edge.shape[2]
    nz = nblk // 2
    pair = 2 * rows
    deep = rows * depth
    chunk = width if deep % width == 0 else deep // 8
    steps = deep // chunk
    edge_flat = edge[0].reshape(deep, width)
    left_flat = proj_left[0].reshape(deep, width)
    right_flat = proj_right[0].reshape(deep, width)

    def whole(*shape):
        return pl.BlockSpec(shape, lambda k: (0,) * len(shape))

    def piece():
        return pl.BlockSpec((chunk, width), lambda k: (jnp.minimum(k, steps - 1), 0))

    anywhere = pl.BlockSpec(memory_space=pl.ANY)

    aligned = rows % 16 == 0
    small = BF16 if aligned else F32
    dma = pltpu.SemaphoreType.DMA
    turned, folded, column, fresh = pl.pallas_call(
        functools.partial(chain_kernel, nsite, nblk, steps),
        grid=(2 * steps,),
        out_shape=(
            jax.ShapeDtypeStruct((2, deep, width), BF16),
            jax.ShapeDtypeStruct((2, width, LANES), BF16),
            jax.ShapeDtypeStruct((width, LANES), F32),
            jax.ShapeDtypeStruct((3, rows, LANES), F32),
        ),
        in_specs=[
            whole(rows, width), piece(), anywhere, anywhere, whole(1, width),
            whole(rows, width), whole(rows, width),
        ],
        out_specs=(anywhere, whole(2, width, LANES), whole(width, LANES), whole(3, rows, LANES)),
        scratch_shapes=[
            pltpu.VMEM((steps, width, chunk), BF16),
            pltpu.VMEM((steps, chunk, width), BF16),
            pltpu.VMEM((steps - steps // 2, chunk, width), BF16),
            pltpu.VMEM((width, width), BF16),
            pltpu.VMEM((width, LANES), BF16),
            pltpu.VMEM((3, chunk, width), BF16),
            pltpu.VMEM((2, width, width), F32),
            pltpu.VMEM((width, width), BF16),
            pltpu.VMEM((width, width), BF16),
            pltpu.VMEM((width, width), BF16),
            pltpu.VMEM((1, 16, LANES) if aligned else (nblk, rows, width), BF16),
            pltpu.VMEM((width, width), BF16),
            pltpu.VMEM((8, width), jnp.int32),
            pltpu.VMEM((8, width), jnp.int32),
            pltpu.VMEM((width, LANES), F32),
            pltpu.VMEM((width, LANES), F32),
            pltpu.VMEM((2, rows, LANES), F32),
            pltpu.VMEM((2, rows, LANES), small),
            pltpu.VMEM((pair, LANES), F32),
            pltpu.VMEM((width, LANES), small),
            pltpu.VMEM((ITERS, width, LANES), BF16),
            pltpu.VMEM((ITERS, width, LANES), BF16),
            pltpu.VMEM((ITERS, nz, pair, LANES), BF16),
            pltpu.VMEM((width, LANES), small),
            pltpu.VMEM((nblk, rows, LANES), small),
            dma((3,)),
            dma((2, nz)), dma((nblk,)),
            dma(()), dma(()),
            dma((nblk,)), dma((nblk,)),
            dma(()), dma(()),
            dma(()), dma(()),
            dma((ITERS, nz)), dma((ITERS, nz)),
            dma((ITERS, nz)), dma((ITERS, nz)),
            dma((nblk,)), dma((nblk,)),
            dma(()), dma(()),
            dma(()), dma(()),
            dma((steps - steps // 2,)),
        ],
        compiler_params=pltpu.CompilerParams(
            collective_id=0, has_side_effects=True, vmem_limit_bytes=VMEM,
            dimension_semantics=("arbitrary",),
        ),
    )(corner[0], edge_flat, left_flat, right_flat, charge, cot_left[0], cot_right[0])
    grad_left, grad_right, new_left, new_right = pl.pallas_call(
        grad_kernel,
        grid=(steps,),
        out_shape=(jax.ShapeDtypeStruct((deep, width), BF16),) * 2
        + (jax.ShapeDtypeStruct((rows, width), BF16),) * 2,
        in_specs=[
            pl.BlockSpec((2, chunk, width), lambda k: (0, k, 0)), whole(2, width, LANES),
            whole(width, LANES), whole(3, rows, LANES), whole(1, width),
        ],
        out_specs=(piece(), piece(), whole(rows, width), whole(rows, width)),
        scratch_shapes=[pltpu.VMEM((2, width, width), BF16)],
        compiler_params=pltpu.CompilerParams(vmem_limit_bytes=VMEM, dimension_semantics=("arbitrary",)),
    )(turned, folded, column, fresh, charge)
    shape = (1, rows, depth, width)
    return (new_left[None], new_right[None], grad_left.reshape(shape), grad_right.reshape(shape))


def solution(mesh):
    placed = (
        P("site", "blk", None),
        P("site", "blk", None, None),
        P("site", "blk", None, None),
        P("site", "blk", None, None),
        P("site", None),
        P("site", "blk", None),
        P("site", "blk", None),
    )
    return jax.shard_map(
        functools.partial(body, mesh.shape["site"], mesh.shape["blk"]),
        mesh=mesh,
        in_specs=placed,
        out_specs=(
            P("site", "blk", None),
            P("site", "blk", None),
            P("site", "blk", None, None),
            P("site", "blk", None, None),
        ),
        check_vma=False,
    )
```

```python
import functools

import jax
import jax.numpy as jnp
from jax import lax
from jax.experimental import pallas as pl
from jax.experimental.pallas import tpu as pltpu
from jax.sharding import PartitionSpec as P

ITERS = 2
LANES = 128
VMEM = 60 * 1024 * 1024
F32 = jnp.float32
BF16 = jnp.bfloat16


def dot(left, right, dims):
    return lax.dot_general(left, right, (dims, ((), ())), preferred_element_type=F32)


def chain_kernel(
    nsite, nblk, steps,
    corner, edge, left, right, labels, cot_left, cot_right,
    turned_out, w_out, col_out, fresh_out,
    ebuf, estore, tbuf, cother, wother, pbuf, acc, snd, rcv, enl, cland, cfull, lab_in, lab_dst, col_own, col_dst, cotf, wsend, cpair,
    wzero, wfull, part, got, newp, newgot,
    f_s, c_s, c_r, l_s, l_r, w_s, w_r, p_s, p_r, e_s, e_r, r_s, r_r, a_s, a_r, n_s, n_r, o_s, o_r, v_s, v_r, t_s,
):
    step = pl.program_id(0)
    rows, width = corner.shape
    nz = nblk // 2
    pair = 2 * rows
    chunk = edge.shape[0]
    aligned = rows % 16 == 0
    blocks = width // LANES
    site = lax.axis_index("site")
    blk = lax.axis_index("blk")
    side = blk % 2
    z = blk // 2
    up = (site + 1) % nsite
    down = (site + nsite - 1) % nsite
    dest = (site + nsite - 1 + 2 * side) % nsite
    origin = (site + nsite + 1 - 2 * side) % nsite
    partner = 2 * z + 1 - side

    def copy(src, dst, send, recv, to_site, to_blk):
        return pltpu.make_async_remote_copy(
            src_ref=src, dst_ref=dst, send_sem=send, recv_sem=recv,
            device_id={"site": to_site, "blk": to_blk}, device_id_type=pl.DeviceIdType.MESH,
        )

    def own_rows(index):
        return pl.ds(pl.multiple_of(index * rows, rows), rows)

    def pair_rows(index):
        return pl.ds(pl.multiple_of(index * pair, pair), pair)

    def corner_slot(index):
        return cfull.at[own_rows(index)] if aligned else cland.at[index]

    def corner_copies():
        there = corner_slot(blk)
        out = []
        for p in range(nz):
            out.append(copy(corner, there, c_s.at[0, p], c_r.at[blk], up, 2 * p))
            out.append(copy(corner, there, c_s.at[1, p], c_r.at[blk], down, 2 * p + 1))
        return out

    def w_copies():
        out = []
        for d in range(1, nblk):
            to = (blk + d) % nblk
            out.append(copy(wsend.at[to % 2], wzero.at[own_rows(blk)], w_s.at[d], w_r.at[blk], site, to))
        return out

    def label_copy():
        return copy(lab_in, lab_dst, l_s, l_r, origin, blk)

    def cot_copy():
        return copy(cotf.at[1 - side], cpair.at[own_rows(side)], p_s, p_r, site, partner)

    def columns(lab, col):
        for i in range(blocks):
            at = slice(i * LANES, (i + 1) * LANES)
            col[at, :] = jnp.broadcast_to(lab[0:1, at].astype(F32), (LANES, LANES)).T

    def same(col_block, lab, j):
        return col_block == lab[0:1, j * LANES:(j + 1) * LANES].astype(F32)

    def fetch(t):
        use_left = (t < steps) == (side == 1)
        here = pl.ds(pl.multiple_of(t % steps * chunk, chunk), chunk)

        @pl.when(use_left)
        def _():
            pltpu.make_async_copy(left.at[here], pbuf.at[t % 3], f_s.at[t % 3]).start()

        @pl.when(jnp.logical_not(use_left))
        def _():
            pltpu.make_async_copy(right.at[here], pbuf.at[t % 3], f_s.at[t % 3]).start()

    @pl.when(step == 0)
    def _():
        fetch(step)
        fetch(step + 1)
        barrier = pltpu.get_barrier_semaphore()
        for where in (down, up):
            for b in range(nblk):
                pl.semaphore_signal(barrier, inc=1, device_id={"site": where, "blk": b}, device_id_type=pl.DeviceIdType.MESH)
        for d in range(1, nblk):
            pl.semaphore_signal(barrier, inc=1, device_id={"site": site, "blk": (blk + d) % nblk}, device_id_type=pl.DeviceIdType.MESH)
        lab_in[...] = jnp.broadcast_to(labels[...], lab_in.shape)
        columns(lab_in, col_own)
        mine = col_own[own_rows(blk), :]
        for s, cot in enumerate((cot_left, cot_right)):
            total = jnp.zeros((rows, LANES), F32)
            for j in range(blocks):
                total = total + jnp.where(same(mine, lab_in, j), cot[:, j * LANES:(j + 1) * LANES], 0.0)
            cotf[s] = total
            wsend[s] = total.astype(BF16).astype(wsend.dtype)
        wzero[own_rows(blk), :] = wsend[side]
        cpair[own_rows(side), :] = cotf[side]
        acc[...] = jnp.zeros_like(acc)

    @pl.when(step == 1)
    def _():
        pl.semaphore_wait(pltpu.get_barrier_semaphore(), 3 * nblk - 1)
        label_copy().start()
        cot_copy().start()
        for c in w_copies() + corner_copies():
            c.start()

    @pl.when(step + 2 < 2 * steps)
    def _():
        fetch(step + 2)

    pltpu.make_async_copy(left.at[pl.ds(0, chunk)], pbuf.at[step % 3], f_s.at[step % 3]).wait()

    @pl.when(step < steps)
    def _():
        turned = edge[...].T
        ebuf[step] = turned
        estore[step] = edge[...]
        acc[0] += dot(turned, pbuf[step % 3], ((1,), (0,)))

    @pl.when(step == steps)
    def _():
        snd[...] = acc[0].astype(BF16)
        copy(snd, rcv, e_s, e_r, site, partner).start()

    @pl.when(step >= steps)
    def _():
        acc[1] += dot(ebuf[step - steps], pbuf[step % 3], ((1,), (0,)))

    def window(i):
        return max(0, i - 1), min(blocks, i + 2)

    def back_partial(at):
        for i in range(blocks):
            rows_i = slice(i * LANES, (i + 1) * LANES)
            lo, hi = window(i)
            span = slice(lo * LANES, hi * LANES)
            folded = wzero[rows_i, :] if at == 0 else wfull[at - 1, rows_i, :]
            mine = col_own[rows_i, :]
            there = col_dst[rows_i, :]
            w = jnp.concatenate(
                [jnp.where(same(mine, lab_in, j), folded.astype(F32), 0.0) for j in range(lo, hi)], axis=1
            ).astype(BF16)
            back = dot(w, enl[span, span], ((1,), (1,)))
            total = jnp.zeros((LANES, LANES), F32)
            for j in range(lo, hi):
                piece = back[:, (j - lo) * LANES:(j - lo + 1) * LANES]
                total = total + jnp.where(same(there, lab_dst, j), piece, 0.0)
            part[at, rows_i, :] = total.astype(BF16)

    def reduce_copies(at):
        return [
            copy(part.at[at, slice_of(p)], got.at[at, z], r_s.at[at, p], r_r.at[at, z], dest, 2 * p + side)
            for p in range(nz)
        ]

    def slice_of(p):
        return pl.ds(p * pair, pair)

    def gather_copies(at):
        here = wfull.at[at, pair_rows(z)]
        return [
            copy(here, here, a_s.at[at, d], a_r.at[at, z], site, 2 * ((z + d) % nz) + side)
            for d in range(1, nz)
        ]

    def reduce_and_send(at):
        for q in range(nz):
            copy(got.at[at, q], got.at[at, q], r_s.at[at, q], r_r.at[at, q], dest, blk).wait_recv()
        total = cpair[...]
        for q in range(nz):
            total = total + got[at, q].astype(F32)
        wfull[at, pair_rows(z), :] = total.astype(BF16)
        for c in gather_copies(at):
            c.start()

    def gather_wait(at):
        for d in range(1, nz):
            src = (z + nz - d) % nz
            there = wfull.at[at, pair_rows(src)]
            copy(there, there, a_s.at[at, d], a_r.at[at, src], site, partner).wait_recv()

    def new_copies():
        out = []
        for d in range(1, nblk):
            to = (blk + d) % nblk
            out.append(copy(newp.at[own_rows(to)], newgot.at[blk], n_s.at[d], n_r.at[blk], site, to))
        return out

    def corner_wait():
        for q in range(nblk):
            there = corner_slot(q)
            copy(there, there, c_s.at[0, 0], c_r.at[q], site, partner).wait_recv()
        if not aligned:
            for q in range(nz):
                both = [cland[2 * q].astype(F32), cland[2 * q + 1].astype(F32)]
                cfull[q * pair:(q + 1) * pair, :] = jnp.concatenate(both, axis=0).astype(BF16)

    def new_partial():
        for i in range(blocks):
            rows_i = slice(i * LANES, (i + 1) * LANES)
            lo, hi = window(i)
            fresh = dot(cfull[rows_i, :], enl[:, lo * LANES:hi * LANES], ((1,), (0,)))
            mine = col_own[rows_i, :]
            total = jnp.zeros((LANES, LANES), F32)
            for j in range(lo, hi):
                piece = fresh[:, (j - lo) * LANES:(j - lo + 1) * LANES]
                total = total + jnp.where(same(mine, lab_in, j), piece, 0.0)
            newp[rows_i, :] = total.astype(newp.dtype)

    halves = (range(0, steps // 2), range(steps // 2, steps))

    def store_copy(which, k, slot):
        return pltpu.make_async_copy(
            tbuf.at[slot], turned_out.at[which, pl.ds(k * chunk, chunk)], t_s.at[slot]
        )

    def edge_corner(which, full, chunks, before):
        for slot, k in enumerate(chunks):
            if before is not None and slot < len(before[1]):
                store_copy(before[0], before[1][slot], slot).wait()
            tbuf[slot] = dot(estore[k], full[...], ((1,), (1,))).astype(BF16)
            store_copy(which, k, slot).start()
        if before is not None:
            for slot in range(len(chunks), len(before[1])):
                store_copy(before[0], before[1][slot], slot).wait()

    @pl.when(step == 2 * steps - 1)
    def _():
        label_copy().wait_recv()
        columns(lab_dst, col_dst)
        cot_copy().wait_recv()
        for d in range(1, nblk):
            src = (blk + nblk - d) % nblk
            there = wzero.at[own_rows(src)]
            copy(there, there, w_s.at[d], w_r.at[src], site, partner).wait_recv()
        swap = copy(snd, rcv, e_s, e_r, site, partner)
        swap.wait_recv()
        enl[...] = (acc[1] + rcv[...].astype(F32)).astype(BF16)
        forward = copy(cfull, cother, o_s, o_r, site, partner)
        w_swap = copy(wfull.at[ITERS - 1], wother, v_s, v_r, site, partner)
        before = None
        for at in range(ITERS):
            if at:
                gather_wait(at - 1)
            back_partial(at)
            for c in reduce_copies(at):
                c.start()
            if at == 0:
                corner_wait()
                forward.start()
                edge_corner(side, cfull, halves[0], before)
                before = (side, halves[0])
            if at == ITERS - 1:
                forward.wait_recv()
                new_partial()
                for c in new_copies():
                    c.start()
                newgot[blk] = newp[own_rows(blk), :]
                edge_corner(1 - side, cother, halves[0], before)
                before = (1 - side, halves[0])
            reduce_and_send(at)
            if at == 0:
                edge_corner(side, cfull, halves[1], before)
                before = (side, halves[1])
            if at == ITERS - 1:
                edge_corner(1 - side, cother, halves[1], before)
                before = (1 - side, halves[1])
        gather_wait(ITERS - 1)
        w_swap.start()
        w_out[side] = wfull[ITERS - 1]
        col_out[...] = col_own[...]
        for d in range(1, nblk):
            src = (blk + nblk - d) % nblk
            copy(newgot.at[src], newgot.at[src], n_s.at[d], n_r.at[src], site, partner).wait_recv()
        for s in range(2):
            total = jnp.zeros((rows, LANES), F32)
            for q in range(nz):
                total = total + newgot[2 * q + s].astype(F32)
            fresh_out[s] = total
        fresh_out[2] = col_own[own_rows(blk), :]
        w_swap.wait_recv()
        w_out[1 - side] = wother[...]
        for slot, k in enumerate(before[1]):
            store_copy(before[0], k, slot).wait()
        w_swap.wait_send()
        forward.wait_send()
        swap.wait_send()
        label_copy().wait_send()
        cot_copy().wait_send()
        for c in w_copies() + corner_copies() + new_copies():
            c.wait_send()
        for at in range(ITERS):
            for c in reduce_copies(at) + gather_copies(at):
                c.wait_send()


def grad_kernel(turned_left, turned_right, folded, column, fresh, labels, grad_left, grad_right, new_left, new_right, wide):
    blocks = labels.shape[1] // LANES
    groups = []
    for j in range(0, blocks, 2):
        top = min(blocks, j + 2)
        groups.append((slice(max(0, j - 1) * LANES, min(blocks, top + 1) * LANES), range(j, top)))

    @pl.when(pl.program_id(0) == 0)
    def _():
        for s in range(2):
            for span, inside in groups:
                for j in inside:
                    at = slice(j * LANES, (j + 1) * LANES)
                    keep = column[span, :] == labels[:, at].astype(F32)
                    wide[s, span, at] = jnp.where(keep, folded[s, span, :].astype(F32), 0.0).astype(BF16)

    for s, (turned, out) in enumerate(((turned_left, grad_left), (turned_right, grad_right))):
        for span, inside in groups:
            here = slice(inside[0] * LANES, (inside[-1] + 1) * LANES)
            out[:, here] = dot(turned[0, :, span], wide[s, span, here], ((1,), (0,))).astype(BF16)

    @pl.when(pl.program_id(0) == 0)
    def _():
        for s, out in enumerate((new_left, new_right)):
            for j in range(labels.shape[1] // LANES):
                at = slice(j * LANES, (j + 1) * LANES)
                keep = fresh[2] == labels[:, at].astype(F32)
                out[:, at] = jnp.where(keep, fresh[s], 0.0).astype(BF16)


def body(nsite, nblk, corner, edge, proj_left, proj_right, charge, cot_left, cot_right):
    rows, width = corner.shape[1:]
    depth = edge.shape[2]
    nz = nblk // 2
    pair = 2 * rows
    deep = rows * depth
    chunk = width if deep % width == 0 else deep // 8
    steps = deep // chunk
    edge_flat = edge[0].reshape(deep, width)
    left_flat = proj_left[0].reshape(deep, width)
    right_flat = proj_right[0].reshape(deep, width)

    def whole(*shape):
        return pl.BlockSpec(shape, lambda k: (0,) * len(shape))

    def piece():
        return pl.BlockSpec((chunk, width), lambda k: (jnp.minimum(k, steps - 1), 0))

    anywhere = pl.BlockSpec(memory_space=pl.ANY)

    aligned = rows % 16 == 0
    small = BF16 if aligned else F32
    dma = pltpu.SemaphoreType.DMA
    turned, folded, column, fresh = pl.pallas_call(
        functools.partial(chain_kernel, nsite, nblk, steps),
        grid=(2 * steps,),
        out_shape=(
            jax.ShapeDtypeStruct((2, deep, width), BF16),
            jax.ShapeDtypeStruct((2, width, LANES), BF16),
            jax.ShapeDtypeStruct((width, LANES), F32),
            jax.ShapeDtypeStruct((3, rows, LANES), F32),
        ),
        in_specs=[
            whole(rows, width), piece(), anywhere, anywhere, whole(1, width),
            whole(rows, width), whole(rows, width),
        ],
        out_specs=(anywhere, whole(2, width, LANES), whole(width, LANES), whole(3, rows, LANES)),
        scratch_shapes=[
            pltpu.VMEM((steps, width, chunk), BF16),
            pltpu.VMEM((steps, chunk, width), BF16),
            pltpu.VMEM((steps - steps // 2, chunk, width), BF16),
            pltpu.VMEM((width, width), BF16),
            pltpu.VMEM((width, LANES), BF16),
            pltpu.VMEM((3, chunk, width), BF16),
            pltpu.VMEM((2, width, width), F32),
            pltpu.VMEM((width, width), BF16),
            pltpu.VMEM((width, width), BF16),
            pltpu.VMEM((width, width), BF16),
            pltpu.VMEM((1, 16, LANES) if aligned else (nblk, rows, width), BF16),
            pltpu.VMEM((width, width), BF16),
            pltpu.VMEM((8, width), jnp.int32),
            pltpu.VMEM((8, width), jnp.int32),
            pltpu.VMEM((width, LANES), F32),
            pltpu.VMEM((width, LANES), F32),
            pltpu.VMEM((2, rows, LANES), F32),
            pltpu.VMEM((2, rows, LANES), small),
            pltpu.VMEM((pair, LANES), F32),
            pltpu.VMEM((width, LANES), small),
            pltpu.VMEM((ITERS, width, LANES), BF16),
            pltpu.VMEM((ITERS, width, LANES), BF16),
            pltpu.VMEM((ITERS, nz, pair, LANES), BF16),
            pltpu.VMEM((width, LANES), small),
            pltpu.VMEM((nblk, rows, LANES), small),
            dma((3,)),
            dma((2, nz)), dma((nblk,)),
            dma(()), dma(()),
            dma((nblk,)), dma((nblk,)),
            dma(()), dma(()),
            dma(()), dma(()),
            dma((ITERS, nz)), dma((ITERS, nz)),
            dma((ITERS, nz)), dma((ITERS, nz)),
            dma((nblk,)), dma((nblk,)),
            dma(()), dma(()),
            dma(()), dma(()),
            dma((steps - steps // 2,)),
        ],
        compiler_params=pltpu.CompilerParams(
            collective_id=0, has_side_effects=True, vmem_limit_bytes=VMEM,
            dimension_semantics=("arbitrary",),
        ),
    )(corner[0], edge_flat, left_flat, right_flat, charge, cot_left[0], cot_right[0])
    slab = 512 if deep % 512 == 0 else chunk
    out_piece = pl.BlockSpec((slab, width), lambda k: (k, 0))
    grad_left, grad_right, new_left, new_right = pl.pallas_call(
        grad_kernel,
        grid=(deep // slab,),
        out_shape=(jax.ShapeDtypeStruct((deep, width), BF16),) * 2
        + (jax.ShapeDtypeStruct((rows, width), BF16),) * 2,
        in_specs=[
            pl.BlockSpec((1, slab, width), lambda k: (0, k, 0)),
            pl.BlockSpec((1, slab, width), lambda k: (1, k, 0)), whole(2, width, LANES),
            whole(width, LANES), whole(3, rows, LANES), whole(1, width),
        ],
        out_specs=(out_piece, out_piece, whole(rows, width), whole(rows, width)),
        scratch_shapes=[pltpu.VMEM((2, width, width), BF16)],
        compiler_params=pltpu.CompilerParams(vmem_limit_bytes=VMEM, dimension_semantics=("arbitrary",)),
    )(turned, turned, folded, column, fresh, charge)
    shape = (1, rows, depth, width)
    return (new_left[None], new_right[None], grad_left.reshape(shape), grad_right.reshape(shape))


def solution(mesh):
    placed = (
        P("site", "blk", None),
        P("site", "blk", None, None),
        P("site", "blk", None, None),
        P("site", "blk", None, None),
        P("site", None),
        P("site", "blk", None),
        P("site", "blk", None),
    )
    return jax.shard_map(
        functools.partial(body, mesh.shape["site"], mesh.shape["blk"]),
        mesh=mesh,
        in_specs=placed,
        out_specs=(
            P("site", "blk", None),
            P("site", "blk", None),
            P("site", "blk", None, None),
            P("site", "blk", None, None),
        ),
        check_vma=False,
    )
```
